32 devices in a mesh: row: 4 (over y, x), col: 8 (over z, core).
Axes of the slice: x: 2, y: 2, z: 4, core: 2. Of those that a mesh axis runs over, the one named last changes fastest.
Arguments:
- tokens: bfloat16 [128, 12288], P('row', 'col'), may hold values from -6 to 6
- grad_out: bfloat16 [128, 12288], P('row', 'col'), may hold values from -1.796875 to 1.796875
- pre_act: bfloat16 [128, 24576], P('col', 'row'), may hold values from -6 to 6
- w_in: bfloat16 [24576, 12288], P('row', 'col'), may hold values from -0.0546875 to 0.0546875
- w_out: bfloat16 [24576, 12288], P('row', 'col'), may hold values from -0.0390625 to 0.0390625
Outputs:
- grad_tokens: bfloat16 [128, 12288], P('row', 'col')
- grad_w_in: bfloat16 [24576, 12288], P('row', 'col')
- grad_w_out: bfloat16 [24576, 12288], P('row', 'col')
The draws below stay inside these ranges and needn't reach their ends.
All inputs are finite; a program needn't handle non-finite values.
Results may differ from the reference program's by a relative error of at most 0.005.
Values may be sent and summed in bfloat16 or wider, within the bound.
No kernel may reach another device: no remote copies, remote signals or barrier semaphores. Data moves between devices by JAX's collectives and lax.ppermute only.
A program may use at most 128 MiB of HBM per device.

```python
import jax
import jax.numpy as jnp
from jax import lax

D = 12288
H = 24576
TOKENS = 128


def block_levels(stream_key, dims, pieces, smallest, largest):
    level = 1.0
    for position, blocks in pieces:
        steps = jax.random.uniform(jax.random.fold_in(jax.random.fold_in(stream_key, 6), position), (blocks,), jnp.float32, smallest / len(pieces), largest / len(pieces))
        level = level * jnp.repeat(jnp.exp(steps), dims[position] // blocks).reshape((-1,) + (1,) * (len(dims) - 1 - position))
    return level


def gaussian(stream_key, extent, deviation, reach, split=(), dtype=jnp.bfloat16):
    entries = jax.random.normal(stream_key, extent, jnp.float32) * deviation
    if len(split) > 0:
        entries = block_levels(stream_key, extent, split, -0.22, 0.18) * entries
    return jnp.clip(entries, min=-reach, max=reach).astype(dtype)


def setup_inputs(seed: int = 0) -> dict:
    splits = jax.random.split(jax.random.key(seed), 6)
    tokens = gaussian(splits[0], (TOKENS, D), 1.0, 6.0, ((0, 4), (1, 8)))
    grad_out = gaussian(splits[1], (TOKENS, D), 0.3, 1.796875, ((0, 4), (1, 8)))
    pre_act = gaussian(splits[2], (TOKENS, H), 1.0, 6.0, ((0, 8), (1, 4)))
    w_in = gaussian(splits[3], (H, D), D ** -0.5, 0.0546875, ((0, 4), (1, 8)))
    w_out = gaussian(splits[4], (H, D), H ** -0.5, 0.0390625, ((0, 4), (1, 8)))
    return dict(tokens=tokens, grad_out=grad_out, pre_act=pre_act, w_in=w_in, w_out=w_out)


tanh_scale = 0.7978845608028654
cubic_term = 0.044715


def gelu_parts(pre_act):
    pre_value = pre_act.astype(jnp.float32)
    tanh_arg = tanh_scale * (pre_value + cubic_term * pre_value * pre_value * pre_value)
    tangent = jnp.tanh(tanh_arg)
    hidden_value = 0.5 * pre_value * (1.0 + tangent)
    gelu_slope = 0.5 * (1.0 + tangent) + 0.5 * pre_value * (1.0 - tangent * tangent) * tanh_scale * (1.0 + 3.0 * cubic_term * pre_value * pre_value)
    return hidden_value, gelu_slope


def reference(tokens, grad_out, pre_act, w_in, w_out):
    contract_rows = (((0,), (0,)), ((), ()))
    contract_cols = (((1,), (1,)), ((), ()))
    grad_hidden = lax.dot_general(grad_out, w_out, contract_cols, preferred_element_type=jnp.float32)
    hidden_value, gelu_slope = gelu_parts(pre_act)
    hidden = hidden_value.astype(jnp.bfloat16)
    grad_pre = (grad_hidden * gelu_slope).astype(jnp.bfloat16)
    grad_tokens = jnp.dot(grad_pre, w_in, preferred_element_type=jnp.float32).astype(jnp.bfloat16)
    grad_w_in = lax.dot_general(grad_pre, tokens, contract_rows, preferred_element_type=jnp.float32).astype(jnp.bfloat16)
    grad_w_out = lax.dot_general(hidden, grad_out, contract_rows, preferred_element_type=jnp.float32).astype(jnp.bfloat16)
    return (grad_tokens, grad_w_in, grad_w_out)
```

```python
import functools

import jax
import jax.numpy as jnp
from jax import lax
from jax.experimental import pallas as pl
from jax.experimental.pallas import tpu as pltpu
from jax.sharding import PartitionSpec as P

tanh_scale = 0.7978845608028654
cubic_term = 0.044715
VMEM_LIMIT = 16 * 1024 * 1024
CHUNKS = 2
AHEAD = 4
FLOPS = 8_000_000_000


def gelu_parts(pre_act):
    pre_value = pre_act.astype(jnp.float32)
    tanh_arg = tanh_scale * (pre_value + cubic_term * pre_value * pre_value * pre_value)
    tangent = jnp.tanh(tanh_arg)
    hidden_value = 0.5 * pre_value * (1.0 + tangent)
    gelu_slope = 0.5 * (1.0 + tangent) + 0.5 * pre_value * (
        1.0 - tangent * tangent
    ) * tanh_scale * (1.0 + 3.0 * cubic_term * pre_value * pre_value)
    return (hidden_value, gelu_slope)


def per_device_any(tokens, grad_out, pre_act, w_in, w_out):
    contract_rows = (((0,), (0,)), ((), ()))
    contract_cols = (((1,), (1,)), ((), ()))
    out_cols = lax.all_gather(grad_out, "row", axis=0, tiled=True)
    grad_hidden = lax.psum_scatter(
        lax.dot_general(out_cols, w_out, contract_cols, preferred_element_type=jnp.float32),
        "col",
        scatter_dimension=0,
        tiled=True,
    )
    hidden_value, gelu_slope = gelu_parts(pre_act)
    grad_pre = (grad_hidden * gelu_slope).astype(jnp.bfloat16)
    hidden_all = lax.all_gather(hidden_value.astype(jnp.bfloat16), "col", axis=0, tiled=True)
    grad_pre_all = lax.all_gather(grad_pre, "col", axis=0, tiled=True)
    grad_w_out = lax.dot_general(
        hidden_all, out_cols, contract_rows, preferred_element_type=jnp.float32
    ).astype(jnp.bfloat16)
    tok_cols = lax.all_gather(tokens, "row", axis=0, tiled=True)
    grad_w_in = lax.dot_general(
        grad_pre_all, tok_cols, contract_rows, preferred_element_type=jnp.float32
    ).astype(jnp.bfloat16)
    grad_tokens = lax.psum_scatter(
        jnp.dot(grad_pre_all, w_in, preferred_element_type=jnp.float32),
        "row",
        scatter_dimension=0,
        tiled=True,
    ).astype(jnp.bfloat16)
    return (grad_tokens, grad_w_in, grad_w_out)


RELATIVE = (0, 2, 1, 3)
ANY = pl.BlockSpec(memory_space=pl.ANY)
VMEM = pl.BlockSpec(memory_space=pltpu.VMEM)
SMEM = pl.BlockSpec(memory_space=pltpu.SMEM)


COST = pl.CostEstimate(flops=FLOPS, bytes_accessed=0, transcendentals=0)
SHORT = pl.CostEstimate(flops=FLOPS // 4, bytes_accessed=0, transcendentals=0)
LIGHT = pl.CostEstimate(flops=FLOPS // 100, bytes_accessed=0, transcendentals=0)


def params(**kw):
    return pltpu.CompilerParams(vmem_limit_bytes=VMEM_LIMIT, **kw)


def swap_rows(array, d):
    return lax.ppermute(array, "row", [(r, r ^ d) for r in range(4)])


def swap_chips(array, d):
    return lax.ppermute(array, "col", [(i, i ^ (2 * d)) for i in range(8)])


def swap_cores(array):
    return lax.ppermute(array, "col", [(i, i ^ 1) for i in range(8)])


def cuts(width, step=256):
    return [slice(n, n + step) for n in range(0, width, step)]


def join_rows(pieces, place, after=()):
    rows, width = pieces[0].shape

    def body(place_ref, p0, p1, p2, p3, *rest):
        place_rows((p0, p1, p2, p3), place_ref, rest[len(after)])

    return pl.pallas_call(
        body,
        out_shape=jax.ShapeDtypeStruct((4 * rows, width), pieces[0].dtype),
        in_specs=[SMEM] + [VMEM] * 4 + [ANY] * len(after),
        out_specs=VMEM,
        compiler_params=params(),
        cost_estimate=LIGHT,
        name="join_rows",
    )(place, *pieces, *after)


def place_rows(pieces, place_ref, out):
    block = pieces[0].shape[0] // 2
    core = place_ref[4]
    for d, piece in enumerate(pieces):
        at = place_ref[d]
        own = pl.multiple_of(core * block, block)
        other = pl.multiple_of((1 - core) * block, block)
        low = pl.multiple_of(at * block, block)
        high = pl.multiple_of((at + 4) * block, block)
        out[pl.ds(low, block), :] = piece[pl.ds(own, block), :]
        out[pl.ds(high, block), :] = piece[pl.ds(other, block), :]


def hidden_grad(x, w_out, first, units, after=(), place=None):
    join = place is not None
    width = w_out.shape[1]
    tokens = 4 * x[0].shape[0] if join else x[0].shape[1]
    half = tokens // 2
    cut = cuts(units)
    pieces = len(x)

    def body(*refs):
        refs = list(refs)
        place_ref = refs.pop(0) if join else None
        x_refs, w_ref = refs[:pieces], refs[pieces]
        own, other, *rest = refs[pieces + 1 + len(after) :]
        held, sems = rest[-2:]
        copies = [
            pltpu.make_async_copy(
                w_ref.at[pl.ds(first + c.start, c.stop - c.start)], held.at[c], sems.at[n]
            )
            for n, c in enumerate(cut)
        ]
        for copy in copies[:AHEAD]:
            copy.start()
        if join:
            joined, flipped = rest[:2]
            place_rows(x_refs, place_ref, joined)
            flipped[...] = joined[...].T
        else:
            flipped = x_refs[0]
        for n, c in enumerate(cut):
            copies[n].wait()
            if n + AHEAD < len(cut):
                copies[n + AHEAD].start()
            value = jnp.dot(held[c, :], flipped[...], preferred_element_type=jnp.float32).T
            own[:, c] = value[:half]
            other[:, c] = value[half:].astype(jnp.bfloat16)

    shapes = [
        jax.ShapeDtypeStruct((half, units), jnp.float32),
        jax.ShapeDtypeStruct((half, units), jnp.bfloat16),
    ]
    if join:
        shapes += [
            jax.ShapeDtypeStruct((tokens, width), jnp.bfloat16),
            jax.ShapeDtypeStruct((width, tokens), jnp.bfloat16),
        ]
    return pl.pallas_call(
        body,
        in_specs=[SMEM] * join + [VMEM] * pieces + [ANY] * (1 + len(after)),
        out_specs=[VMEM] * len(shapes),
        out_shape=shapes,
        scratch_shapes=[
            pltpu.VMEM((units, width), jnp.bfloat16),
            pltpu.SemaphoreType.DMA((len(cut),)),
        ],
        compiler_params=params(),
        cost_estimate=LIGHT if join else COST,
        name="hidden_grad",
    )(*([place] if join else []), *x, w_out, *after)


def add(own, got):
    return own[...] + got[...].astype(jnp.float32)


def halve(value, held, send):
    keep = held.shape[0]
    held[...] = value[:keep]
    send[...] = value[keep:].astype(jnp.bfloat16)


def slope_times(value, pre_ref, first):
    units = value.shape[1]
    slope = gelu_parts(pre_ref[:, first * units : (first + 1) * units])[1]
    return (value * slope).astype(jnp.bfloat16)


def small(body, operands, shapes, after=(), cost=COST, name="small"):
    inputs = len(operands)

    def call(*refs):
        body(*refs[:inputs], *refs[inputs + len(after) :])

    return pl.pallas_call(
        call,
        out_shape=[jax.ShapeDtypeStruct(shape, kind) for shape, kind in shapes],
        in_specs=[VMEM] * inputs + [ANY] * len(after),
        out_specs=[VMEM] * len(shapes),
        compiler_params=params(),
        cost_estimate=cost,
        name=name,
    )(*operands, *after)


def sum_cores(own, got, after=()):
    rows, units = own.shape
    half = (rows // 2, units)

    def body(own, got, held, send):
        halve(add(own, got), held, send)

    return small(
        body, [own, got], [(half, jnp.float32), (half, jnp.bfloat16)], after, name="sum_cores"
    )


def sum_near(held0, near0, own1, core1, after=()):
    rows, units = own1.shape
    half, quarter = (rows // 2, units), (rows // 4, units)

    def body(held0, near0, own1, core1, mine0, send0, held1, send1):
        halve(add(held0, near0), mine0, send0)
        halve(add(own1, core1), held1, send1)

    return small(
        body,
        [held0, near0, own1, core1],
        [
            (quarter, jnp.float32),
            (quarter, jnp.bfloat16),
            (half, jnp.float32),
            (half, jnp.bfloat16),
        ],
        after,
        name="sum_near",
    )


def sum_far(mine0, far0, held1, near1, pre_act, after=()):
    quarter = mine0.shape

    def body(mine0, far0, held1, near1, pre_ref, grad0, mine1, send1):
        grad0[...] = slope_times(add(mine0, far0), pre_ref, 0)
        halve(add(held1, near1), mine1, send1)

    return small(
        body,
        [mine0, far0, held1, near1, pre_act],
        [(quarter, jnp.bfloat16), (quarter, jnp.float32), (quarter, jnp.bfloat16)],
        after,
        name="sum_far",
    )


def pair_far(grad0, far0, mine1, far1, pre_act, pre_most, pre_last, after=()):
    rows, units = grad0.shape
    most, wide = pre_most.shape

    def body(grad0, far0, mine1, far1, pre_ref, pre_most, pre_last, pair0, grad1, pre_own):
        pair0[:rows] = grad0[...]
        pair0[rows:] = far0[...]
        grad1[...] = slope_times(add(mine1, far1), pre_ref, 1)
        pre_own[:most] = pre_most[...]
        pre_own[most:] = pre_last[...]

    return small(
        body,
        [grad0, far0, mine1, far1, pre_act, pre_most, pre_last],
        [
            ((2 * rows, units), jnp.bfloat16),
            ((rows, units), jnp.bfloat16),
            ((most + rows, wide), jnp.bfloat16),
        ],
        after,
        name="pair_far",
    )


def pair_near(near0, grad1, far1, after=()):
    rows, units = grad1.shape

    def body(near0, grad1, far1, blocks0, pair1):
        blocks0[...] = near0[...]
        pair1[:rows] = grad1[...]
        pair1[rows:] = far1[...]

    return small(
        body,
        [near0, grad1, far1],
        [(near0.shape, jnp.bfloat16), ((2 * rows, units), jnp.bfloat16)],
        after,
        LIGHT,
        "pair_near",
    )


def out_weight_grad(pre, x, first, rows, held, after=()):
    tokens, width = x.shape
    units = pre[0].shape[1]
    pieces = len(pre)
    extra = len(after) + (held is not None)
    parts = cuts(rows)

    def body(*refs):
        pre_refs, x_ref = refs[:pieces], refs[pieces]
        out, token, stage, sems = refs[pieces + 1 + extra :]
        copies = []
        for n, part in enumerate(parts):
            some = slice(first + part.start, first + part.stop)
            value = jnp.concatenate([ref[:, some] for ref in pre_refs], axis=0)
            value = value.astype(jnp.float32)
            tangent = jnp.tanh(tanh_scale * (value + cubic_term * value * value * value))
            hidden = (0.5 * value * (1.0 + tangent)).astype(jnp.bfloat16).T
            for cut in cuts(width):
                stage[part, cut] = jnp.dot(
                    hidden, x_ref[:, cut], preferred_element_type=jnp.float32
                ).astype(jnp.bfloat16)
            copies.append(pltpu.make_async_copy(stage.at[part], out.at[some], sems.at[n]))
            copies[-1].start()
        token[...] = jnp.zeros_like(token)
        for copy in copies:
            copy.wait()

    operands = [*pre, x] + ([] if held is None else [held]) + list(after)
    return pl.pallas_call(
        body,
        in_specs=[VMEM] * (pieces + 1) + [ANY] * extra,
        out_specs=[ANY, VMEM],
        out_shape=[
            jax.ShapeDtypeStruct((units, width), jnp.bfloat16),
            jax.ShapeDtypeStruct((8, 128), jnp.float32),
        ],
        scratch_shapes=[
            pltpu.VMEM((rows, width), jnp.bfloat16),
            pltpu.SemaphoreType.DMA((len(parts),)),
        ],
        input_output_aliases={} if held is None else {pieces + 1: 0},
        compiler_params=params(),
        cost_estimate=COST,
        name="out_weight_grad",
    )(*operands)


def in_grads(grad_pre, w_in, tok, first, count, rows, held, total, place, after=()):
    tokens, width = tok.shape
    block = tokens // 8
    pieces = len(grad_pre)
    start, last = total is None, place is not None

    def body(*refs):
        refs = list(refs)
        place_ref = refs.pop(0) if last else None
        w_ref, tok_ref = refs[pieces : pieces + 2]
        if last:
            out, parts, sums = refs[-6], refs[-5:-1], refs[-1]
        else:
            out, sums = refs[-2:]
        value = jnp.concatenate([ref[...] for ref in refs[:pieces]], axis=0)

        @pl.when(pl.program_id(0) == 0)
        def _():
            sums[...] = jnp.zeros_like(sums) if start else refs[pieces + 3][...]

        here = pl.multiple_of((first + pl.program_id(0)) * rows, rows)
        sums[...] += jnp.dot(
            value, w_ref[pl.ds(here, rows), :], preferred_element_type=jnp.float32
        )
        for some in cuts(rows):
            flipped = value[:, some].T
            for cut in cuts(width):
                out[some, cut] = jnp.dot(
                    flipped, tok_ref[:, cut], preferred_element_type=jnp.float32
                ).astype(jnp.bfloat16)

        if last:

            @pl.when(pl.program_id(0) == count - 1)
            def _():
                core = place_ref[4]
                for d, part in enumerate(parts):
                    low = pl.multiple_of((place_ref[d] + 4 * core) * block, block)
                    high = pl.multiple_of((place_ref[d] + 4 * (1 - core)) * block, block)
                    part[:block] = sums[pl.ds(low, block), :].astype(part.dtype)
                    part[block:] = sums[pl.ds(high, block), :].astype(part.dtype)

    whole = pl.BlockSpec((tokens, width), lambda i: (0, 0))
    in_specs = [pl.BlockSpec((p.shape[0], rows), lambda i: (0, i)) for p in grad_pre]
    in_specs += [
        VMEM,
        whole,
    ]
    operands = [*grad_pre, w_in, tok]
    if not start:
        in_specs += [ANY, whole]
        operands += [held, total]
    in_specs += [ANY] * len(after)
    operands += after
    out_specs = [pl.BlockSpec((rows, width), lambda i: (first + i, 0))]
    out_shape = [jax.ShapeDtypeStruct(w_in.shape, jnp.bfloat16)]
    scratch = []
    if last:
        in_specs = [SMEM] + in_specs
        operands = [place] + operands
        out_specs += [pl.BlockSpec((2 * block, width), lambda i: (0, 0))] * 4
        out_shape += [
            jax.ShapeDtypeStruct((2 * block, width), kind)
            for kind in (jnp.float32, jnp.bfloat16, jnp.bfloat16, jnp.bfloat16)
        ]
        scratch = [pltpu.VMEM((tokens, width), jnp.float32)]
    else:
        out_specs.append(whole)
        out_shape.append(jax.ShapeDtypeStruct((tokens, width), jnp.float32))
    return pl.pallas_call(
        body,
        grid=(count,),
        in_specs=in_specs,
        out_specs=out_specs,
        out_shape=out_shape,
        scratch_shapes=scratch,
        input_output_aliases={} if start else {pieces + 2 + last: 0},
        compiler_params=params(),
        cost_estimate=COST,
        name="in_grads",
    )(*operands)


def mark(after=(), cost=SHORT):
    def body(*refs):
        refs[-1][...] = jnp.zeros_like(refs[-1])

    return pl.pallas_call(
        body,
        out_shape=jax.ShapeDtypeStruct((8, 128), jnp.float32),
        in_specs=[ANY] * len(after),
        out_specs=VMEM,
        compiler_params=params(),
        cost_estimate=cost,
        name="mark",
    )(*after)


def tie(value, after, cost=LIGHT):
    def body(*refs):
        pass

    return pl.pallas_call(
        body,
        out_shape=jax.ShapeDtypeStruct(value.shape, value.dtype),
        in_specs=[ANY] * (1 + len(after)),
        out_specs=ANY,
        input_output_aliases={0: 0},
        compiler_params=params(),
        cost_estimate=cost,
        name="tie",
    )(value, *after)


def stack(pieces, after=()):
    rows, units = pieces[0].shape
    count = len(pieces)

    def body(*refs):
        for n in range(count):
            refs[-1][n * rows : (n + 1) * rows] = refs[n][...]

    return pl.pallas_call(
        body,
        out_shape=jax.ShapeDtypeStruct((count * rows, units), pieces[0].dtype),
        in_specs=[VMEM] * count + [ANY] * len(after),
        out_specs=VMEM,
        compiler_params=params(),
        cost_estimate=COST,
        name="stack",
    )(*pieces, *after)


def per_device_line(tokens, grad_out, pre_act, w_in, w_out):
    row = lax.axis_index("row")
    col = lax.axis_index("col")
    chip, core = col // 2, col % 2
    apart = [chip ^ row ^ d for d in range(4)]
    spots = [2 * (v & 1) + v // 2 for v in apart]
    place = jnp.stack(spots + [core]).astype(jnp.int32)

    units = w_out.shape[0]
    rows = 512
    per_chunk = units // CHUNKS
    count = per_chunk // rows

    started = mark()
    for _ in range(7):
        started = mark((started,))
    w_out = pltpu.with_memory_space_constraint(w_out, pltpu.HBM)
    pre_far, pre_near = swap_chips(pre_act, 2), swap_chips(pre_act, 1)
    own0, send0, x, flipped = hidden_grad(
        [grad_out] + [swap_rows(grad_out, d) for d in (1, 2, 3)],
        w_out,
        0,
        per_chunk,
        (started,),
        place,
    )
    pre_most = stack([pre_act, pre_far, pre_near], (send0,))
    step = mark((pre_most,), COST)
    held0, out0 = sum_cores(own0, swap_cores(send0), (step,))
    own1, send1 = hidden_grad([flipped], w_out, per_chunk, per_chunk, (out0,))
    mine = stack([tokens], (send1,))
    mine0, out0, held1, out1 = sum_near(
        held0, swap_chips(out0, 1), own1, swap_cores(send1), (mine,)
    )
    grad0, mine1, out1 = sum_far(
        mine0, swap_chips(out0, 2), held1, swap_chips(out1, 1), pre_act
    )
    tok = join_rows([mine] + [swap_rows(mine, d) for d in (1, 2, 3)], place, (grad0,))
    pair0, grad1, pre_own = pair_far(
        grad0,
        swap_chips(grad0, 2),
        mine1,
        swap_chips(out1, 2),
        pre_act,
        pre_most,
        swap_chips(pre_far, 1),
        (tok,),
    )
    pre = [pre_own, swap_cores(pre_own)]
    grad_w_out, token = out_weight_grad(pre, x, 0, units // 2, None, (pair0,))
    near0, pair1 = pair_near(swap_chips(pair0, 1), grad1, swap_chips(grad1, 2), (token,))
    whole = [pair0, near0, swap_cores(pair0), swap_cores(near0)]
    grad_w_in, total = in_grads(
        whole, w_in, tok, 0, count // 2, 2 * rows, None, None, None, (pair1,)
    )
    near1 = tie(swap_chips(pair1, 1), (total,))
    whole = [pair1, near1, swap_cores(pair1), swap_cores(near1)]
    grad_w_in, part, *parts = in_grads(
        whole, w_in, tok, count // 2, count // 2, 2 * rows, grad_w_in, total, place
    )
    grad_w_out, _ = out_weight_grad(pre, x, units // 2, units // 2, grad_w_out, (part,))
    for d in (1, 2, 3):
        part = part + swap_rows(parts[d - 1], d).astype(jnp.float32)
    return (part.astype(jnp.bfloat16), grad_w_in, grad_w_out)


def solution(mesh):
    line = mesh.shape["row"] == 4 and mesh.shape["col"] == 8
    in_specs = (P("row", "col"), P("row", "col"), P("col", "row"), P("row", "col"), P("row", "col"))
    out_specs = (P("row", "col"), P("row", "col"), P("row", "col"))
    return jax.shard_map(
        per_device_line if line else per_device_any,
        mesh=mesh,
        in_specs=in_specs,
        out_specs=out_specs,
        check_vma=False,
    )
```

```python
import functools

import jax
import jax.numpy as jnp
from jax import lax
from jax.experimental import pallas as pl
from jax.experimental.pallas import tpu as pltpu
from jax.sharding import PartitionSpec as P

tanh_scale = 0.7978845608028654
cubic_term = 0.044715
VMEM_LIMIT = 16 * 1024 * 1024
CHUNKS = 2
FLOPS = 8_000_000_000


def gelu_parts(pre_act):
    pre_value = pre_act.astype(jnp.float32)
    tanh_arg = tanh_scale * (pre_value + cubic_term * pre_value * pre_value * pre_value)
    tangent = jnp.tanh(tanh_arg)
    hidden_value = 0.5 * pre_value * (1.0 + tangent)
    gelu_slope = 0.5 * (1.0 + tangent) + 0.5 * pre_value * (
        1.0 - tangent * tangent
    ) * tanh_scale * (1.0 + 3.0 * cubic_term * pre_value * pre_value)
    return (hidden_value, gelu_slope)


def per_device_any(tokens, grad_out, pre_act, w_in, w_out):
    contract_rows = (((0,), (0,)), ((), ()))
    contract_cols = (((1,), (1,)), ((), ()))
    out_cols = lax.all_gather(grad_out, "row", axis=0, tiled=True)
    grad_hidden = lax.psum_scatter(
        lax.dot_general(out_cols, w_out, contract_cols, preferred_element_type=jnp.float32),
        "col",
        scatter_dimension=0,
        tiled=True,
    )
    hidden_value, gelu_slope = gelu_parts(pre_act)
    grad_pre = (grad_hidden * gelu_slope).astype(jnp.bfloat16)
    hidden_all = lax.all_gather(hidden_value.astype(jnp.bfloat16), "col", axis=0, tiled=True)
    grad_pre_all = lax.all_gather(grad_pre, "col", axis=0, tiled=True)
    grad_w_out = lax.dot_general(
        hidden_all, out_cols, contract_rows, preferred_element_type=jnp.float32
    ).astype(jnp.bfloat16)
    tok_cols = lax.all_gather(tokens, "row", axis=0, tiled=True)
    grad_w_in = lax.dot_general(
        grad_pre_all, tok_cols, contract_rows, preferred_element_type=jnp.float32
    ).astype(jnp.bfloat16)
    grad_tokens = lax.psum_scatter(
        jnp.dot(grad_pre_all, w_in, preferred_element_type=jnp.float32),
        "row",
        scatter_dimension=0,
        tiled=True,
    ).astype(jnp.bfloat16)
    return (grad_tokens, grad_w_in, grad_w_out)


RELATIVE = (0, 2, 1, 3)
ANY = pl.BlockSpec(memory_space=pl.ANY)
VMEM = pl.BlockSpec(memory_space=pltpu.VMEM)
SMEM = pl.BlockSpec(memory_space=pltpu.SMEM)


COST = pl.CostEstimate(flops=FLOPS, bytes_accessed=0, transcendentals=0)
SHORT = pl.CostEstimate(flops=FLOPS // 4, bytes_accessed=0, transcendentals=0)
LIGHT = pl.CostEstimate(flops=FLOPS // 100, bytes_accessed=0, transcendentals=0)


def params(**kw):
    return pltpu.CompilerParams(vmem_limit_bytes=VMEM_LIMIT, **kw)


def swap_rows(array, d):
    return lax.ppermute(array, "row", [(r, r ^ d) for r in range(4)])


def swap_chips(array, d):
    return lax.ppermute(array, "col", [(i, i ^ (2 * d)) for i in range(8)])


def swap_cores(array):
    return lax.ppermute(array, "col", [(i, i ^ 1) for i in range(8)])


def cuts(width, step=256):
    return [slice(n, n + step) for n in range(0, width, step)]


def join_rows(pieces, place, after=()):
    rows, width = pieces[0].shape

    def body(place_ref, p0, p1, p2, p3, *rest):
        place_rows((p0, p1, p2, p3), place_ref, rest[len(after)])

    return pl.pallas_call(
        body,
        out_shape=jax.ShapeDtypeStruct((4 * rows, width), pieces[0].dtype),
        in_specs=[SMEM] + [VMEM] * 4 + [ANY] * len(after),
        out_specs=VMEM,
        compiler_params=params(),
        cost_estimate=LIGHT,
        name="join_rows",
    )(place, *pieces, *after)


def place_rows(pieces, place_ref, out):
    block = pieces[0].shape[0] // 2
    core = place_ref[4]
    for d, piece in enumerate(pieces):
        at = place_ref[d]
        own = pl.multiple_of(core * block, block)
        other = pl.multiple_of((1 - core) * block, block)
        low = pl.multiple_of(at * block, block)
        high = pl.multiple_of((at + 4) * block, block)
        out[pl.ds(low, block), :] = piece[pl.ds(own, block), :]
        out[pl.ds(high, block), :] = piece[pl.ds(other, block), :]


def hidden_grad(x, w_out, first, units, after=(), place=None):
    join = place is not None
    width = w_out.shape[1]
    tokens = 4 * x[0].shape[0] if join else x[0].shape[1]
    half = tokens // 2
    bounds = [units * n // 12 for n in (0, 3, 6, 8, 10, 11, 12)]
    cut = [slice(a, b) for a, b in zip(bounds[:-1], bounds[1:])]
    groups = [cut[n : n + 2] for n in (0, 2, 4)]
    pieces = len(x)

    def body(*refs):
        refs = list(refs)
        place_ref = refs.pop(0) if join else None
        x_refs, w_ref = refs[:pieces], refs[pieces]
        own, other, *rest = refs[pieces + 1 + len(after) :]
        held, sems = rest[-2:]
        copies = [
            pltpu.make_async_copy(
                w_ref.at[pl.ds(first + c.start, c.stop - c.start)], held.at[c], sems.at[n]
            )
            for n, c in enumerate(cut)
        ]
        for copy in copies[:2]:
            copy.start()
        if join:
            joined, flipped = rest[:2]
            place_rows(x_refs, place_ref, joined)
            flipped[...] = joined[...].T
        else:
            flipped = x_refs[0]
        for n, group in enumerate(groups):
            for copy in copies[2 * n : 2 * n + 2]:
                copy.wait()
            for copy in copies[2 * n + 2 : 2 * n + 4]:
                copy.start()
            for c in cuts(group[1].stop - group[0].start, 512):
                c = slice(group[0].start + c.start, group[0].start + c.stop)
                value = jnp.dot(held[c, :], flipped[...], preferred_element_type=jnp.float32).T
                own[:, c] = value[:half]
                other[:, c] = value[half:].astype(jnp.bfloat16)

    shapes = [
        jax.ShapeDtypeStruct((half, units), jnp.float32),
        jax.ShapeDtypeStruct((half, units), jnp.bfloat16),
    ]
    if join:
        shapes += [
            jax.ShapeDtypeStruct((tokens, width), jnp.bfloat16),
            jax.ShapeDtypeStruct((width, tokens), jnp.bfloat16),
        ]
    return pl.pallas_call(
        body,
        in_specs=[SMEM] * join + [VMEM] * pieces + [ANY] * (1 + len(after)),
        out_specs=[VMEM] * len(shapes),
        out_shape=shapes,
        scratch_shapes=[
            pltpu.VMEM((units, width), jnp.bfloat16),
            pltpu.SemaphoreType.DMA((len(cut),)),
        ],
        compiler_params=params(),
        cost_estimate=LIGHT if join else COST,
        name="hidden_grad",
    )(*([place] if join else []), *x, w_out, *after)


def add(own, got):
    return own[...] + got[...].astype(jnp.float32)


def halve(value, held, send):
    keep = held.shape[0]
    held[...] = value[:keep]
    send[...] = value[keep:].astype(jnp.bfloat16)


def slope_times(value, pre_ref, first):
    units = value.shape[1]
    slope = gelu_parts(pre_ref[:, first * units : (first + 1) * units])[1]
    return (value * slope).astype(jnp.bfloat16)


def small(body, operands, shapes, after=(), cost=COST, name="small"):
    inputs = len(operands)

    def call(*refs):
        body(*refs[:inputs], *refs[inputs + len(after) :])

    return pl.pallas_call(
        call,
        out_shape=[jax.ShapeDtypeStruct(shape, kind) for shape, kind in shapes],
        in_specs=[VMEM] * inputs + [ANY] * len(after),
        out_specs=[VMEM] * len(shapes),
        compiler_params=params(),
        cost_estimate=cost,
        name=name,
    )(*operands, *after)


def sum_cores(own, got, after=()):
    rows, units = own.shape
    half = (rows // 2, units)

    def body(own, got, held, send):
        halve(add(own, got), held, send)

    return small(
        body, [own, got], [(half, jnp.float32), (half, jnp.bfloat16)], after, name="sum_cores"
    )


def sum_near(held0, near0, own1, core1, after=()):
    rows, units = own1.shape
    half, quarter = (rows // 2, units), (rows // 4, units)

    def body(held0, near0, own1, core1, mine0, send0, held1, send1):
        halve(add(held0, near0), mine0, send0)
        halve(add(own1, core1), held1, send1)

    return small(
        body,
        [held0, near0, own1, core1],
        [
            (quarter, jnp.float32),
            (quarter, jnp.bfloat16),
            (half, jnp.float32),
            (half, jnp.bfloat16),
        ],
        after,
        name="sum_near",
    )


def sum_far(mine0, far0, held1, near1, pre_act, after=()):
    quarter = mine0.shape

    def body(mine0, far0, held1, near1, pre_ref, grad0, mine1, send1):
        grad0[...] = slope_times(add(mine0, far0), pre_ref, 0)
        halve(add(held1, near1), mine1, send1)

    return small(
        body,
        [mine0, far0, held1, near1, pre_act],
        [(quarter, jnp.bfloat16), (quarter, jnp.float32), (quarter, jnp.bfloat16)],
        after,
        name="sum_far",
    )


def pair_far(grad0, far0, mine1, far1, pre_act, after=()):
    rows, units = grad0.shape

    def body(grad0, far0, mine1, far1, pre_ref, pair0, grad1):
        pair0[:rows] = grad0[...]
        pair0[rows:] = far0[...]
        grad1[...] = slope_times(add(mine1, far1), pre_ref, 1)

    return small(
        body,
        [grad0, far0, mine1, far1, pre_act],
        [((2 * rows, units), jnp.bfloat16), ((rows, units), jnp.bfloat16)],
        after,
        name="pair_far",
    )


def pair_near(near0, grad1, far1, after=()):
    rows, units = grad1.shape

    def body(near0, grad1, far1, blocks0, pair1):
        blocks0[...] = near0[...]
        pair1[:rows] = grad1[...]
        pair1[rows:] = far1[...]

    return small(
        body,
        [near0, grad1, far1],
        [(near0.shape, jnp.bfloat16), ((2 * rows, units), jnp.bfloat16)],
        after,
        LIGHT,
        "pair_near",
    )


def weight_grad(pieces, x, first, start, rows, units, held, activate, after=()):
    tokens, width = x.shape
    count = len(pieces)
    extra = len(after) + (held is not None)
    parts = cuts(rows, 512)

    def body(*refs):
        a_refs, x_ref = refs[:count], refs[count]
        out, token, stage, sems = refs[count + 1 + extra :]
        copies = []
        for n, part in enumerate(parts):
            for here in cuts(part.stop - part.start):
                low = start + part.start + here.start
                high = start + part.start + here.stop
                a = jnp.concatenate([ref[:, low:high] for ref in a_refs], axis=0)
                if activate:
                    value = a.astype(jnp.float32)
                    cube = cubic_term * value * value * value
                    tangent = jnp.tanh(tanh_scale * (value + cube))
                    a = (0.5 * value * (1.0 + tangent)).astype(jnp.bfloat16)
                a = a.T
                for cut in cuts(width):
                    stage[low - start : high - start, cut] = jnp.dot(
                        a, x_ref[:, cut], preferred_element_type=jnp.float32
                    ).astype(jnp.bfloat16)
            there = pl.ds(first + start + part.start, part.stop - part.start)
            copies.append(pltpu.make_async_copy(stage.at[part], out.at[there], sems.at[n]))
            copies[-1].start()
        token[...] = jnp.zeros_like(token)
        for copy in copies:
            copy.wait()

    operands = [*pieces, x] + ([] if held is None else [held]) + list(after)
    return pl.pallas_call(
        body,
        in_specs=[VMEM] * (count + 1) + [ANY] * extra,
        out_specs=[ANY, VMEM],
        out_shape=[
            jax.ShapeDtypeStruct((units, width), jnp.bfloat16),
            jax.ShapeDtypeStruct((8, 128), jnp.float32),
        ],
        scratch_shapes=[
            pltpu.VMEM((rows, width), jnp.bfloat16),
            pltpu.SemaphoreType.DMA((len(parts),)),
        ],
        input_output_aliases={} if held is None else {count + 1: 0},
        compiler_params=params(),
        cost_estimate=COST,
        name="out_weight_grad" if activate else "in_weight_grad",
    )(*operands)


def token_grad(pieces, w_in, first, total, place, after=()):
    count = len(pieces)
    tokens, units = count * pieces[0].shape[0], pieces[0].shape[1]
    width = w_in.shape[1]
    block = tokens // 8
    last, more = place is not None, total is not None

    def body(*refs):
        refs = list(refs)
        place_ref = refs.pop(0) if last else None
        w_ref = refs[count]
        outs = refs[count + 1 + more + len(after) :]
        sums = outs[-1]
        value = jnp.concatenate([ref[...] for ref in refs[:count]], axis=0)
        for n, some in enumerate(cuts(units, 1024)):
            part = jnp.dot(
                value[:, some],
                w_ref[first + some.start : first + some.stop, :],
                preferred_element_type=jnp.float32,
            )
            if n > 0:
                sums[...] += part
            else:
                sums[...] = part + refs[count + 1][...] if more else part
        if last:
            core = place_ref[4]
            for d, part in enumerate(outs[:4]):
                low = pl.multiple_of((place_ref[d] + 4 * core) * block, block)
                high = pl.multiple_of((place_ref[d] + 4 * (1 - core)) * block, block)
                part[:block] = sums[pl.ds(low, block), :].astype(part.dtype)
                part[block:] = sums[pl.ds(high, block), :].astype(part.dtype)

    shapes = [jax.ShapeDtypeStruct((tokens, width), jnp.float32)]
    if last:
        shapes = [
            jax.ShapeDtypeStruct((2 * block, width), kind)
            for kind in (jnp.float32, jnp.bfloat16, jnp.bfloat16, jnp.bfloat16)
        ]
    return pl.pallas_call(
        body,
        in_specs=[SMEM] * last + [VMEM] * (count + 1 + more) + [ANY] * len(after),
        out_specs=[VMEM] * len(shapes),
        out_shape=shapes,
        scratch_shapes=[pltpu.VMEM((tokens, width), jnp.float32)] if last else [],
        compiler_params=params(),
        cost_estimate=COST,
        name="token_grad",
    )(*([place] if last else []), *pieces, w_in, *([total] if more else []), *after)


def mark(after=(), cost=SHORT):
    def body(*refs):
        refs[-1][...] = jnp.zeros_like(refs[-1])

    return pl.pallas_call(
        body,
        out_shape=jax.ShapeDtypeStruct((8, 128), jnp.float32),
        in_specs=[ANY] * len(after),
        out_specs=VMEM,
        compiler_params=params(),
        cost_estimate=cost,
        name="mark",
    )(*after)


def tie(value, after, cost=LIGHT):
    def body(*refs):
        pass

    return pl.pallas_call(
        body,
        out_shape=jax.ShapeDtypeStruct(value.shape, value.dtype),
        in_specs=[ANY] * (1 + len(after)),
        out_specs=ANY,
        input_output_aliases={0: 0},
        compiler_params=params(),
        cost_estimate=cost,
        name="tie",
    )(value, *after)


def stack(pieces, after=()):
    rows, units = pieces[0].shape
    count = len(pieces)

    def body(*refs):
        for n in range(count):
            refs[-1][n * rows : (n + 1) * rows] = refs[n][...]

    return pl.pallas_call(
        body,
        out_shape=jax.ShapeDtypeStruct((count * rows, units), pieces[0].dtype),
        in_specs=[VMEM] * count + [ANY] * len(after),
        out_specs=VMEM,
        compiler_params=params(),
        cost_estimate=COST,
        name="stack",
    )(*pieces, *after)


def per_device_line(tokens, grad_out, pre_act, w_in, w_out):
    row = lax.axis_index("row")
    col = lax.axis_index("col")
    chip, core = col // 2, col % 2
    apart = [chip ^ row ^ d for d in range(4)]
    spots = [2 * (v & 1) + v // 2 for v in apart]
    place = jnp.stack(spots + [core]).astype(jnp.int32)

    units = w_out.shape[0]
    per_chunk = units // CHUNKS

    started = mark()
    for _ in range(7):
        started = mark((started,))
    w_out = pltpu.with_memory_space_constraint(w_out, pltpu.HBM)
    pre_far, pre_near = swap_chips(pre_act, 2), swap_chips(pre_act, 1)
    own0, send0, x, flipped = hidden_grad(
        [grad_out] + [swap_rows(grad_out, d) for d in (1, 2, 3)],
        w_out,
        0,
        per_chunk,
        (started,),
        place,
    )
    pre_most = stack([pre_act, pre_far, pre_near], (send0,))
    step = mark((pre_most,), COST)
    held0, out0 = sum_cores(own0, swap_cores(send0), (step,))
    own1, send1 = hidden_grad([flipped], w_out, per_chunk, per_chunk, (out0,))
    mine = stack([tokens], (send1,))
    mine0, out0, held1, out1 = sum_near(
        held0, swap_chips(out0, 1), own1, swap_cores(send1), (mine,)
    )
    pre_own = stack([pre_act, pre_far, pre_near, swap_chips(pre_far, 1)], (out1,))
    pre = [pre_own, swap_cores(pre_own)]
    grad0, mine1, out1 = sum_far(
        mine0, swap_chips(out0, 2), held1, swap_chips(out1, 1), pre_act, (pre_own,)
    )
    tok = join_rows([mine] + [swap_rows(mine, d) for d in (1, 2, 3)], place, (grad0,))
    half = units // 2
    grad_w_out, token = weight_grad(pre, x, 0, 0, half, units, None, True, (tok,))
    pair0, grad1 = pair_far(
        grad0, swap_chips(grad0, 2), mine1, swap_chips(out1, 2), pre_act, (token,)
    )
    grad_w_out, token = weight_grad(pre, x, 0, half, half, units, grad_w_out, True, (pair0,))
    near0, pair1 = pair_near(swap_chips(pair0, 1), grad1, swap_chips(grad1, 2), (token,))
    whole = [pair0, near0, swap_cores(pair0), swap_cores(near0)]
    grad_w_in, token = weight_grad(whole, tok, 0, 0, per_chunk, units, None, False, (pair1,))
    near1 = tie(swap_chips(pair1, 1), (token,))
    (total,) = token_grad(whole, w_in, 0, None, None, (near1,))
    whole = [pair1, near1, swap_cores(pair1), swap_cores(near1)]
    part, *parts = token_grad(whole, w_in, per_chunk, total, place)
    grad_w_in, _ = weight_grad(
        whole, tok, per_chunk, 0, per_chunk, units, grad_w_in, False, (part,)
    )
    for d in (1, 2, 3):
        part = part + swap_rows(parts[d - 1], d).astype(jnp.float32)
    return (part.astype(jnp.bfloat16), grad_w_in, grad_w_out)


def solution(mesh):
    line = mesh.shape["row"] == 4 and mesh.shape["col"] == 8
    in_specs = (P("row", "col"), P("row", "col"), P("col", "row"), P("row", "col"), P("row", "col"))
    out_specs = (P("row", "col"), P("row", "col"), P("row", "col"))
    return jax.shard_map(
        per_device_line if line else per_device_any,
        mesh=mesh,
        in_specs=in_specs,
        out_specs=out_specs,
        check_vma=False,
    )
```

```python
import functools

import jax
import jax.numpy as jnp
from jax import lax
from jax.experimental import pallas as pl
from jax.experimental.pallas import tpu as pltpu
from jax.sharding import PartitionSpec as P

tanh_scale = 0.7978845608028654
cubic_term = 0.044715
VMEM_LIMIT = 16 * 1024 * 1024
CHUNKS = 2
AHEAD = 3
FLOPS = 8_000_000_000


def gelu_parts(pre_act):
    pre_value = pre_act.astype(jnp.float32)
    tanh_arg = tanh_scale * (pre_value + cubic_term * pre_value * pre_value * pre_value)
    tangent = jnp.tanh(tanh_arg)
    hidden_value = 0.5 * pre_value * (1.0 + tangent)
    gelu_slope = 0.5 * (1.0 + tangent) + 0.5 * pre_value * (
        1.0 - tangent * tangent
    ) * tanh_scale * (1.0 + 3.0 * cubic_term * pre_value * pre_value)
    return (hidden_value, gelu_slope)


def per_device_any(tokens, grad_out, pre_act, w_in, w_out):
    contract_rows = (((0,), (0,)), ((), ()))
    contract_cols = (((1,), (1,)), ((), ()))
    out_cols = lax.all_gather(grad_out, "row", axis=0, tiled=True)
    grad_hidden = lax.psum_scatter(
        lax.dot_general(out_cols, w_out, contract_cols, preferred_element_type=jnp.float32),
        "col",
        scatter_dimension=0,
        tiled=True,
    )
    hidden_value, gelu_slope = gelu_parts(pre_act)
    grad_pre = (grad_hidden * gelu_slope).astype(jnp.bfloat16)
    hidden_all = lax.all_gather(hidden_value.astype(jnp.bfloat16), "col", axis=0, tiled=True)
    grad_pre_all = lax.all_gather(grad_pre, "col", axis=0, tiled=True)
    grad_w_out = lax.dot_general(
        hidden_all, out_cols, contract_rows, preferred_element_type=jnp.float32
    ).astype(jnp.bfloat16)
    tok_cols = lax.all_gather(tokens, "row", axis=0, tiled=True)
    grad_w_in = lax.dot_general(
        grad_pre_all, tok_cols, contract_rows, preferred_element_type=jnp.float32
    ).astype(jnp.bfloat16)
    grad_tokens = lax.psum_scatter(
        jnp.dot(grad_pre_all, w_in, preferred_element_type=jnp.float32),
        "row",
        scatter_dimension=0,
        tiled=True,
    ).astype(jnp.bfloat16)
    return (grad_tokens, grad_w_in, grad_w_out)


RELATIVE = (0, 2, 1, 3)
ANY = pl.BlockSpec(memory_space=pl.ANY)
VMEM = pl.BlockSpec(memory_space=pltpu.VMEM)
SMEM = pl.BlockSpec(memory_space=pltpu.SMEM)


COST = pl.CostEstimate(flops=FLOPS, bytes_accessed=0, transcendentals=0)
SHORT = pl.CostEstimate(flops=FLOPS // 4, bytes_accessed=0, transcendentals=0)
LIGHT = pl.CostEstimate(flops=FLOPS // 100, bytes_accessed=0, transcendentals=0)


def params(**kw):
    return pltpu.CompilerParams(vmem_limit_bytes=VMEM_LIMIT, **kw)


def swap_rows(array, d):
    return lax.ppermute(array, "row", [(r, r ^ d) for r in range(4)])


def swap_chips(array, d):
    return lax.ppermute(array, "col", [(i, i ^ (2 * d)) for i in range(8)])


def swap_cores(array):
    return lax.ppermute(array, "col", [(i, i ^ 1) for i in range(8)])


def cuts(width, step=256):
    return [slice(n, n + step) for n in range(0, width, step)]


def join_rows(pieces, place, after=()):
    rows, width = pieces[0].shape

    def body(place_ref, p0, p1, p2, p3, *rest):
        place_rows((p0, p1, p2, p3), place_ref, rest[len(after)])

    return pl.pallas_call(
        body,
        out_shape=jax.ShapeDtypeStruct((4 * rows, width), pieces[0].dtype),
        in_specs=[SMEM] + [VMEM] * 4 + [ANY] * len(after),
        out_specs=VMEM,
        compiler_params=params(),
        cost_estimate=LIGHT,
        name="join_rows",
    )(place, *pieces, *after)


def place_rows(pieces, place_ref, out):
    block = pieces[0].shape[0] // 2
    core = place_ref[4]
    for d, piece in enumerate(pieces):
        at = place_ref[d]
        own = pl.multiple_of(core * block, block)
        other = pl.multiple_of((1 - core) * block, block)
        low = pl.multiple_of(at * block, block)
        high = pl.multiple_of((at + 4) * block, block)
        out[pl.ds(low, block), :] = piece[pl.ds(own, block), :]
        out[pl.ds(high, block), :] = piece[pl.ds(other, block), :]


def hidden_grad(x, w_out, first, units, after=(), place=None):
    join = place is not None
    width = w_out.shape[1]
    tokens = 4 * x[0].shape[0] if join else x[0].shape[1]
    half = tokens // 2
    cut = cuts(units, 512)
    groups = [cut[n : n + 2] for n in range(1, len(cut) - 1, 2)]
    groups = [cut[:1]] + groups + [cut[-1:]]
    pieces = len(x)

    def body(*refs):
        refs = list(refs)
        place_ref = refs.pop(0) if join else None
        x_refs, w_ref = refs[:pieces], refs[pieces]
        own, other, *rest = refs[pieces + 1 + len(after) :]
        held, sems = rest[-2:]
        copies = [
            pltpu.make_async_copy(
                w_ref.at[pl.ds(first + c.start, c.stop - c.start)], held.at[c], sems.at[n]
            )
            for n, c in enumerate(cut)
        ]
        for copy in copies[:AHEAD]:
            copy.start()
        if join:
            joined, flipped = rest[:2]
            place_rows(x_refs, place_ref, joined)
            flipped[...] = joined[...].T
        else:
            flipped = x_refs[0]
        arrived = 0
        for group in groups:
            for copy in copies[arrived : arrived + len(group)]:
                copy.wait()
            for copy in copies[arrived + AHEAD : arrived + AHEAD + len(group)]:
                copy.start()
            arrived += len(group)
            for c in group:
                value = jnp.dot(held[c, :], flipped[...], preferred_element_type=jnp.float32).T
                own[:, c] = value[:half]
                other[:, c] = value[half:].astype(jnp.bfloat16)

    shapes = [
        jax.ShapeDtypeStruct((half, units), jnp.float32),
        jax.ShapeDtypeStruct((half, units), jnp.bfloat16),
    ]
    if join:
        shapes += [
            jax.ShapeDtypeStruct((tokens, width), jnp.bfloat16),
            jax.ShapeDtypeStruct((width, tokens), jnp.bfloat16),
        ]
    return pl.pallas_call(
        body,
        in_specs=[SMEM] * join + [VMEM] * pieces + [ANY] * (1 + len(after)),
        out_specs=[VMEM] * len(shapes),
        out_shape=shapes,
        scratch_shapes=[
            pltpu.VMEM((units, width), jnp.bfloat16),
            pltpu.SemaphoreType.DMA((len(cut),)),
        ],
        compiler_params=params(),
        cost_estimate=LIGHT if join else COST,
        name="hidden_grad",
    )(*([place] if join else []), *x, w_out, *after)


def add(own, got):
    return own[...] + got[...].astype(jnp.float32)


def halve(value, held, send):
    keep = held.shape[0]
    held[...] = value[:keep]
    send[...] = value[keep:].astype(jnp.bfloat16)


def slope_times(value, pre_ref, first):
    units = value.shape[1]
    slope = gelu_parts(pre_ref[:, first * units : (first + 1) * units])[1]
    return (value * slope).astype(jnp.bfloat16)


def small(body, operands, shapes, after=(), cost=COST, name="small"):
    inputs = len(operands)

    def call(*refs):
        body(*refs[:inputs], *refs[inputs + len(after) :])

    return pl.pallas_call(
        call,
        out_shape=[jax.ShapeDtypeStruct(shape, kind) for shape, kind in shapes],
        in_specs=[VMEM] * inputs + [ANY] * len(after),
        out_specs=[VMEM] * len(shapes),
        compiler_params=params(),
        cost_estimate=cost,
        name=name,
    )(*operands, *after)


def add_halves(own, got, after=(), cost=COST):
    rows, units = own.shape
    half = (rows // 2, units)

    def body(own, got, held, send):
        halve(add(own, got), held, send)

    return small(
        body, [own, got], [(half, jnp.float32), (half, jnp.bfloat16)], after, cost, "add_halves"
    )


def sum_near(held0, near0, own1, core1, after=()):
    rows, units = own1.shape
    half, quarter = (rows // 2, units), (rows // 4, units)

    def body(held0, near0, own1, core1, mine0, send0, held1, send1):
        halve(add(held0, near0), mine0, send0)
        halve(add(own1, core1), held1, send1)

    return small(
        body,
        [held0, near0, own1, core1],
        [
            (quarter, jnp.float32),
            (quarter, jnp.bfloat16),
            (half, jnp.float32),
            (half, jnp.bfloat16),
        ],
        after,
        name="sum_near",
    )


def far_slope(mine, far, pre_act, chunk, after=(), cost=LIGHT):
    def body(mine, far, pre_ref, grad):
        grad[...] = slope_times(add(mine, far), pre_ref, chunk)

    shapes = [(mine.shape, jnp.bfloat16)]
    return small(body, [mine, far, pre_act], shapes, after, cost, "far_slope")[0]


def weight_grad(
    pieces, x, first, start, rows, units, held, activate, after=(), cost=COST
):
    tokens, width = x.shape
    count = len(pieces)
    extra = len(after) + (held is not None)
    parts = cuts(rows, 512)

    def body(*refs):
        a_refs, x_ref = refs[:count], refs[count]
        out, token, stage, sems = refs[count + 1 + extra :]
        copies = []
        for n, part in enumerate(parts):
            for here in cuts(part.stop - part.start):
                low = start + part.start + here.start
                high = start + part.start + here.stop
                a = jnp.concatenate([ref[:, low:high] for ref in a_refs], axis=0)
                if activate:
                    value = a.astype(jnp.float32)
                    cube = cubic_term * value * value * value
                    tangent = jnp.tanh(tanh_scale * (value + cube))
                    a = (0.5 * value * (1.0 + tangent)).astype(jnp.bfloat16)
                a = a.T
                for cut in cuts(width):
                    stage[low - start : high - start, cut] = jnp.dot(
                        a, x_ref[:, cut], preferred_element_type=jnp.float32
                    ).astype(jnp.bfloat16)
            there = pl.ds(first + start + part.start, part.stop - part.start)
            copies.append(pltpu.make_async_copy(stage.at[part], out.at[there], sems.at[n]))
            copies[-1].start()
        token[...] = jnp.zeros_like(token)
        for copy in copies:
            copy.wait()

    operands = [*pieces, x] + ([] if held is None else [held]) + list(after)
    return pl.pallas_call(
        body,
        in_specs=[VMEM] * (count + 1) + [ANY] * extra,
        out_specs=[ANY, VMEM],
        out_shape=[
            jax.ShapeDtypeStruct((units, width), jnp.bfloat16),
            jax.ShapeDtypeStruct((8, 128), jnp.float32),
        ],
        scratch_shapes=[
            pltpu.VMEM((rows, width), jnp.bfloat16),
            pltpu.SemaphoreType.DMA((len(parts),)),
        ],
        input_output_aliases={} if held is None else {count + 1: 0},
        compiler_params=params(),
        cost_estimate=cost,
        name="out_weight_grad" if activate else "in_weight_grad",
    )(*operands)


def token_grad(pieces, w_in, first, total, place, after=()):
    count = len(pieces)
    tokens, units = count * pieces[0].shape[0], pieces[0].shape[1]
    width = w_in.shape[1]
    block = tokens // 8
    last, more = place is not None, total is not None

    def body(*refs):
        refs = list(refs)
        place_ref = refs.pop(0) if last else None
        w_ref = refs[count]
        outs = refs[count + 1 + more + len(after) :]
        sums = outs[-1]
        value = jnp.concatenate([ref[...] for ref in refs[:count]], axis=0)
        for n, some in enumerate(cuts(units, 1024)):
            part = jnp.dot(
                value[:, some],
                w_ref[first + some.start : first + some.stop, :],
                preferred_element_type=jnp.float32,
            )
            if n > 0:
                sums[...] += part
            else:
                sums[...] = part + refs[count + 1][...] if more else part
        if last:
            core = place_ref[4]
            for d, part in enumerate(outs[:4]):
                low = pl.multiple_of((place_ref[d] + 4 * core) * block, block)
                high = pl.multiple_of((place_ref[d] + 4 * (1 - core)) * block, block)
                part[:block] = sums[pl.ds(low, block), :].astype(part.dtype)
                part[block:] = sums[pl.ds(high, block), :].astype(part.dtype)

    shapes = [jax.ShapeDtypeStruct((tokens, width), jnp.float32)]
    if last:
        shapes = [
            jax.ShapeDtypeStruct((2 * block, width), kind)
            for kind in (jnp.float32, jnp.bfloat16, jnp.bfloat16, jnp.bfloat16)
        ]
    return pl.pallas_call(
        body,
        in_specs=[SMEM] * last + [VMEM] * (count + 1 + more) + [ANY] * len(after),
        out_specs=[VMEM] * len(shapes),
        out_shape=shapes,
        scratch_shapes=[pltpu.VMEM((tokens, width), jnp.float32)] if last else [],
        compiler_params=params(),
        cost_estimate=COST,
        name="token_grad",
    )(*([place] if last else []), *pieces, w_in, *([total] if more else []), *after)


def mark(after=(), cost=SHORT, held=()):
    def body(*refs):
        refs[-1][...] = jnp.zeros_like(refs[-1])

    return pl.pallas_call(
        body,
        out_shape=jax.ShapeDtypeStruct((8, 128), jnp.float32),
        in_specs=[ANY] * len(after) + [VMEM] * len(held),
        out_specs=VMEM,
        compiler_params=params(),
        cost_estimate=cost,
        name="mark",
    )(*after, *held)


def tie(value, after, cost=LIGHT):
    def body(*refs):
        pass

    return pl.pallas_call(
        body,
        out_shape=jax.ShapeDtypeStruct(value.shape, value.dtype),
        in_specs=[ANY] * (1 + len(after)),
        out_specs=ANY,
        input_output_aliases={0: 0},
        compiler_params=params(),
        cost_estimate=cost,
        name="tie",
    )(value, *after)


def stack(pieces, after=()):
    rows, units = pieces[0].shape
    count = len(pieces)

    def body(*refs):
        for n in range(count):
            refs[-1][n * rows : (n + 1) * rows] = refs[n][...]

    return pl.pallas_call(
        body,
        out_shape=jax.ShapeDtypeStruct((count * rows, units), pieces[0].dtype),
        in_specs=[VMEM] * count + [ANY] * len(after),
        out_specs=VMEM,
        compiler_params=params(),
        cost_estimate=COST,
        name="stack",
    )(*pieces, *after)


def per_device_line(tokens, grad_out, pre_act, w_in, w_out):
    row = lax.axis_index("row")
    col = lax.axis_index("col")
    chip, core = col // 2, col % 2
    apart = [chip ^ row ^ d for d in range(4)]
    spots = [2 * (v & 1) + v // 2 for v in apart]
    place = jnp.stack(spots + [core]).astype(jnp.int32)

    units = w_out.shape[0]
    per_chunk = units // CHUNKS

    started = mark()
    for _ in range(7):
        started = mark((started,))
    w_out = pltpu.with_memory_space_constraint(w_out, pltpu.HBM)
    pre_far, pre_near = swap_chips(pre_act, 2), swap_chips(pre_act, 1)
    own0, send0, x, flipped = hidden_grad(
        [grad_out] + [swap_rows(grad_out, d) for d in (1, 2, 3)],
        w_out,
        0,
        per_chunk,
        (started,),
        place,
    )
    pre_most = stack([pre_act, pre_far, pre_near], (send0,))
    step = mark((pre_most,), COST)
    held0, out0 = add_halves(own0, swap_cores(send0), (step,))
    own1, send1 = hidden_grad([flipped], w_out, per_chunk, per_chunk, (out0,))
    mine = stack([tokens], (send1,))
    mine0, out0, held1, out1 = sum_near(
        held0, swap_chips(out0, 1), own1, swap_cores(send1), (mine,)
    )
    pre_own = stack([pre_act, pre_far, pre_near, swap_chips(pre_far, 1)], (out1,))
    pre = [pre_own, swap_cores(pre_own)]
    grad0 = far_slope(mine0, swap_chips(out0, 2), pre_act, 0, (pre_own,), COST)
    mine1, out1 = add_halves(held1, swap_chips(out1, 1), (grad0,), LIGHT)
    ends = [units * n // 12 for n in (0, 2, 7, 11, 12)]
    parts = [b - a for a, b in zip(ends[:-1], ends[1:])]
    grad_w_out, token = weight_grad(pre, x, 0, 0, parts[0], units, None, True, (out1,), LIGHT)
    pair0 = stack([grad0, swap_chips(grad0, 2)], (token,))
    grad_w_out, token = weight_grad(
        pre, x, 0, ends[1], parts[1], units, grad_w_out, True, (pair0,)
    )
    tok = join_rows([mine] + [swap_rows(mine, d) for d in (1, 2, 3)], place, (token,))
    grad1 = far_slope(mine1, swap_chips(out1, 2), pre_act, 1, (tok,))
    near0 = tie(swap_chips(pair0, 1), (grad1,))
    whole = [pair0, near0, swap_cores(pair0), swap_cores(near0)]
    step = mark((near0,), LIGHT, (w_in,))
    grad_w_in, token = weight_grad(
        whole, tok, 0, 0, per_chunk, units, None, False, (step,), LIGHT
    )
    pair1 = stack([grad1, swap_chips(grad1, 2)], (token,))
    grad_w_out, token = weight_grad(
        pre, x, 0, ends[2], parts[2], units, grad_w_out, True, (pair1,), LIGHT
    )
    (total,) = token_grad(whole, w_in, 0, None, None, (token,))
    near1 = tie(swap_chips(pair1, 1), (total,))
    whole = [pair1, near1, swap_cores(pair1), swap_cores(near1)]
    grad_w_out, token = weight_grad(
        pre, x, 0, ends[3], parts[3], units, grad_w_out, True, (near1,)
    )
    part, *parts = token_grad(whole, w_in, per_chunk, total, place, (token,))
    grad_w_in, _ = weight_grad(
        whole, tok, per_chunk, 0, per_chunk, units, grad_w_in, False, (part,)
    )
    for d in (1, 2, 3):
        part = part + swap_rows(parts[d - 1], d).astype(jnp.float32)
    return (part.astype(jnp.bfloat16), grad_w_in, grad_w_out)


def solution(mesh):
    line = mesh.shape["row"] == 4 and mesh.shape["col"] == 8
    in_specs = (P("row", "col"), P("row", "col"), P("col", "row"), P("row", "col"), P("row", "col"))
    out_specs = (P("row", "col"), P("row", "col"), P("row", "col"))
    return jax.shard_map(
        per_device_line if line else per_device_any,
        mesh=mesh,
        in_specs=in_specs,
        out_specs=out_specs,
        check_vma=False,
    )
```

```python
import functools

import jax
import jax.numpy as jnp
from jax import lax
from jax.experimental import pallas as pl
from jax.experimental.pallas import tpu as pltpu
from jax.sharding import PartitionSpec as P

tanh_scale = 0.7978845608028654
cubic_term = 0.044715
VMEM_LIMIT = 16 * 1024 * 1024
CHUNKS = 2
AHEAD = 3
FLOPS = 8_000_000_000


def gelu_parts(pre_act):
    pre_value = pre_act.astype(jnp.float32)
    tanh_arg = tanh_scale * (pre_value + cubic_term * pre_value * pre_value * pre_value)
    tangent = jnp.tanh(tanh_arg)
    hidden_value = 0.5 * pre_value * (1.0 + tangent)
    gelu_slope = 0.5 * (1.0 + tangent) + 0.5 * pre_value * (
        1.0 - tangent * tangent
    ) * tanh_scale * (1.0 + 3.0 * cubic_term * pre_value * pre_value)
    return (hidden_value, gelu_slope)


def per_device_any(tokens, grad_out, pre_act, w_in, w_out):
    contract_rows = (((0,), (0,)), ((), ()))
    contract_cols = (((1,), (1,)), ((), ()))
    out_cols = lax.all_gather(grad_out, "row", axis=0, tiled=True)
    grad_hidden = lax.psum_scatter(
        lax.dot_general(out_cols, w_out, contract_cols, preferred_element_type=jnp.float32),
        "col",
        scatter_dimension=0,
        tiled=True,
    )
    hidden_value, gelu_slope = gelu_parts(pre_act)
    grad_pre = (grad_hidden * gelu_slope).astype(jnp.bfloat16)
    hidden_all = lax.all_gather(hidden_value.astype(jnp.bfloat16), "col", axis=0, tiled=True)
    grad_pre_all = lax.all_gather(grad_pre, "col", axis=0, tiled=True)
    grad_w_out = lax.dot_general(
        hidden_all, out_cols, contract_rows, preferred_element_type=jnp.float32
    ).astype(jnp.bfloat16)
    tok_cols = lax.all_gather(tokens, "row", axis=0, tiled=True)
    grad_w_in = lax.dot_general(
        grad_pre_all, tok_cols, contract_rows, preferred_element_type=jnp.float32
    ).astype(jnp.bfloat16)
    grad_tokens = lax.psum_scatter(
        jnp.dot(grad_pre_all, w_in, preferred_element_type=jnp.float32),
        "row",
        scatter_dimension=0,
        tiled=True,
    ).astype(jnp.bfloat16)
    return (grad_tokens, grad_w_in, grad_w_out)


RELATIVE = (0, 2, 1, 3)
ANY = pl.BlockSpec(memory_space=pl.ANY)
VMEM = pl.BlockSpec(memory_space=pltpu.VMEM)
SMEM = pl.BlockSpec(memory_space=pltpu.SMEM)


COST = pl.CostEstimate(flops=FLOPS, bytes_accessed=0, transcendentals=0)
SHORT = pl.CostEstimate(flops=FLOPS // 4, bytes_accessed=0, transcendentals=0)
LIGHT = pl.CostEstimate(flops=FLOPS // 100, bytes_accessed=0, transcendentals=0)


def params(**kw):
    return pltpu.CompilerParams(vmem_limit_bytes=VMEM_LIMIT, **kw)


def swap_rows(array, d):
    return lax.ppermute(array, "row", [(r, r ^ d) for r in range(4)])


def swap_chips(array, d):
    return lax.ppermute(array, "col", [(i, i ^ (2 * d)) for i in range(8)])


def swap_cores(array):
    return lax.ppermute(array, "col", [(i, i ^ 1) for i in range(8)])


def cuts(width, step=256):
    return [slice(n, n + step) for n in range(0, width, step)]


def join_rows(pieces, place, after=()):
    rows, width = pieces[0].shape

    def body(place_ref, p0, p1, p2, p3, *rest):
        place_rows((p0, p1, p2, p3), place_ref, rest[len(after)])

    return pl.pallas_call(
        body,
        out_shape=jax.ShapeDtypeStruct((4 * rows, width), pieces[0].dtype),
        in_specs=[SMEM] + [VMEM] * 4 + [ANY] * len(after),
        out_specs=VMEM,
        compiler_params=params(),
        cost_estimate=LIGHT,
        name="join_rows",
    )(place, *pieces, *after)


def place_rows(pieces, place_ref, out):
    block = pieces[0].shape[0] // 2
    core = place_ref[4]
    for d, piece in enumerate(pieces):
        at = place_ref[d]
        own = pl.multiple_of(core * block, block)
        other = pl.multiple_of((1 - core) * block, block)
        low = pl.multiple_of(at * block, block)
        high = pl.multiple_of((at + 4) * block, block)
        out[pl.ds(low, block), :] = piece[pl.ds(own, block), :]
        out[pl.ds(high, block), :] = piece[pl.ds(other, block), :]


def hidden_grad(x, w_out, first, units, after=(), place=None):
    join = place is not None
    width = w_out.shape[1]
    tokens = 4 * x[0].shape[0] if join else x[0].shape[1]
    half = tokens // 2
    cut = cuts(units, 512)
    groups = [cut[n : n + 2] for n in range(1, len(cut) - 1, 2)]
    groups = [cut[:1]] + groups + [cut[-1:]]
    pieces = len(x)

    def body(*refs):
        refs = list(refs)
        place_ref = refs.pop(0) if join else None
        x_refs, w_ref = refs[:pieces], refs[pieces]
        own, other, *rest = refs[pieces + 1 + len(after) :]
        held, sems = rest[-2:]
        copies = [
            pltpu.make_async_copy(
                w_ref.at[pl.ds(first + c.start, c.stop - c.start)], held.at[c], sems.at[n]
            )
            for n, c in enumerate(cut)
        ]
        for copy in copies[:AHEAD]:
            copy.start()
        if join:
            joined, flipped = rest[:2]
            place_rows(x_refs, place_ref, joined)
            flipped[...] = joined[...].T
        else:
            flipped = x_refs[0]
        arrived = 0
        for group in groups:
            for copy in copies[arrived : arrived + len(group)]:
                copy.wait()
            for copy in copies[arrived + AHEAD : arrived + AHEAD + len(group)]:
                copy.start()
            arrived += len(group)
            for c in group:
                value = jnp.dot(held[c, :], flipped[...], preferred_element_type=jnp.float32).T
                own[:, c] = value[:half]
                other[:, c] = value[half:].astype(jnp.bfloat16)

    shapes = [
        jax.ShapeDtypeStruct((half, units), jnp.float32),
        jax.ShapeDtypeStruct((half, units), jnp.bfloat16),
    ]
    if join:
        shapes += [
            jax.ShapeDtypeStruct((tokens, width), jnp.bfloat16),
            jax.ShapeDtypeStruct((width, tokens), jnp.bfloat16),
        ]
    return pl.pallas_call(
        body,
        in_specs=[SMEM] * join + [VMEM] * pieces + [ANY] * (1 + len(after)),
        out_specs=[VMEM] * len(shapes),
        out_shape=shapes,
        scratch_shapes=[
            pltpu.VMEM((units, width), jnp.bfloat16),
            pltpu.SemaphoreType.DMA((len(cut),)),
        ],
        compiler_params=params(),
        cost_estimate=LIGHT if join else COST,
        name="hidden_grad",
    )(*([place] if join else []), *x, w_out, *after)


def add(own, got):
    return own[...] + got[...].astype(jnp.float32)


def halve(value, held, send):
    keep = held.shape[0]
    held[...] = value[:keep]
    send[...] = value[keep:].astype(jnp.bfloat16)


def slope_times(value, pre_ref, first):
    units = value.shape[1]
    slope = gelu_parts(pre_ref[:, first * units : (first + 1) * units])[1]
    return (value * slope).astype(jnp.bfloat16)


def small(body, operands, shapes, after=(), cost=COST, name="small"):
    inputs = len(operands)

    def call(*refs):
        body(*refs[:inputs], *refs[inputs + len(after) :])

    return pl.pallas_call(
        call,
        out_shape=[jax.ShapeDtypeStruct(shape, kind) for shape, kind in shapes],
        in_specs=[VMEM] * inputs + [ANY] * len(after),
        out_specs=[VMEM] * len(shapes),
        compiler_params=params(),
        cost_estimate=cost,
        name=name,
    )(*operands, *after)


def add_halves(own, got, after=(), cost=COST):
    rows, units = own.shape
    half = (rows // 2, units)

    def body(own, got, held, send):
        halve(add(own, got), held, send)

    return small(
        body, [own, got], [(half, jnp.float32), (half, jnp.bfloat16)], after, cost, "add_halves"
    )


def sum_near(held0, near0, own1, core1, after=()):
    rows, units = own1.shape
    half, quarter = (rows // 2, units), (rows // 4, units)

    def body(held0, near0, own1, core1, mine0, send0, held1, send1):
        halve(add(held0, near0), mine0, send0)
        halve(add(own1, core1), held1, send1)

    return small(
        body,
        [held0, near0, own1, core1],
        [
            (quarter, jnp.float32),
            (quarter, jnp.bfloat16),
            (half, jnp.float32),
            (half, jnp.bfloat16),
        ],
        after,
        name="sum_near",
    )


def far_slope(mine, far, pre_act, chunk, after=(), cost=LIGHT):
    def body(mine, far, pre_ref, grad):
        grad[...] = slope_times(add(mine, far), pre_ref, chunk)

    shapes = [(mine.shape, jnp.bfloat16)]
    return small(body, [mine, far, pre_act], shapes, after, cost, "far_slope")[0]


def weight_grad(
    pieces, x, first, start, rows, units, held, activate, after=(), cost=COST
):
    tokens, width = x.shape
    count = len(pieces)
    extra = len(after) + (held is not None)
    parts = cuts(rows, 512)
    low, high = parts[-1].start, parts[-1].stop
    parts = parts[:-1] + [slice(low, high - 256), slice(high - 256, high)]

    def body(*refs):
        a_refs, x_ref = refs[:count], refs[count]
        out, token, stage, sems = refs[count + 1 + extra :]
        copies = []
        for n, part in enumerate(parts):
            for here in cuts(part.stop - part.start):
                low = start + part.start + here.start
                high = start + part.start + here.stop
                a = jnp.concatenate([ref[:, low:high] for ref in a_refs], axis=0)
                if activate:
                    value = a.astype(jnp.float32)
                    cube = cubic_term * value * value * value
                    tangent = jnp.tanh(tanh_scale * (value + cube))
                    a = (0.5 * value * (1.0 + tangent)).astype(jnp.bfloat16)
                a = a.T
                for cut in cuts(width):
                    stage[low - start : high - start, cut] = jnp.dot(
                        a, x_ref[:, cut], preferred_element_type=jnp.float32
                    ).astype(jnp.bfloat16)
            there = pl.ds(first + start + part.start, part.stop - part.start)
            copies.append(pltpu.make_async_copy(stage.at[part], out.at[there], sems.at[n]))
            copies[-1].start()
        token[...] = jnp.zeros_like(token)
        for copy in copies:
            copy.wait()

    operands = [*pieces, x] + ([] if held is None else [held]) + list(after)
    return pl.pallas_call(
        body,
        in_specs=[VMEM] * (count + 1) + [ANY] * extra,
        out_specs=[ANY, VMEM],
        out_shape=[
            jax.ShapeDtypeStruct((units, width), jnp.bfloat16),
            jax.ShapeDtypeStruct((8, 128), jnp.float32),
        ],
        scratch_shapes=[
            pltpu.VMEM((rows, width), jnp.bfloat16),
            pltpu.SemaphoreType.DMA((len(parts),)),
        ],
        input_output_aliases={} if held is None else {count + 1: 0},
        compiler_params=params(),
        cost_estimate=cost,
        name="out_weight_grad" if activate else "in_weight_grad",
    )(*operands)


def token_grad(pieces, w_in, first, total, place, after=()):
    count = len(pieces)
    tokens, units = count * pieces[0].shape[0], pieces[0].shape[1]
    width = w_in.shape[1]
    block = tokens // 8
    last, more = place is not None, total is not None

    def body(*refs):
        refs = list(refs)
        place_ref = refs.pop(0) if last else None
        w_ref = refs[count]
        outs = refs[count + 1 + more + len(after) :]
        sums = outs[-1]
        value = jnp.concatenate([ref[...] for ref in refs[:count]], axis=0)
        for n, some in enumerate(cuts(units, 1024)):
            part = jnp.dot(
                value[:, some],
                w_ref[first + some.start : first + some.stop, :],
                preferred_element_type=jnp.float32,
            )
            if n > 0:
                sums[...] += part
            else:
                sums[...] = part + refs[count + 1][...] if more else part
        if last:
            core = place_ref[4]
            for d, part in enumerate(outs[:4]):
                low = pl.multiple_of((place_ref[d] + 4 * core) * block, block)
                high = pl.multiple_of((place_ref[d] + 4 * (1 - core)) * block, block)
                part[:block] = sums[pl.ds(low, block), :].astype(part.dtype)
                part[block:] = sums[pl.ds(high, block), :].astype(part.dtype)

    shapes = [jax.ShapeDtypeStruct((tokens, width), jnp.float32)]
    if last:
        shapes = [
            jax.ShapeDtypeStruct((2 * block, width), kind)
            for kind in (jnp.float32, jnp.bfloat16, jnp.bfloat16, jnp.bfloat16)
        ]
    return pl.pallas_call(
        body,
        in_specs=[SMEM] * last + [VMEM] * (count + 1 + more) + [ANY] * len(after),
        out_specs=[VMEM] * len(shapes),
        out_shape=shapes,
        scratch_shapes=[pltpu.VMEM((tokens, width), jnp.float32)] if last else [],
        compiler_params=params(),
        cost_estimate=COST,
        name="token_grad",
    )(*([place] if last else []), *pieces, w_in, *([total] if more else []), *after)


def mark(after=(), cost=SHORT, held=()):
    def body(*refs):
        refs[-1][...] = jnp.zeros_like(refs[-1])

    return pl.pallas_call(
        body,
        out_shape=jax.ShapeDtypeStruct((8, 128), jnp.float32),
        in_specs=[ANY] * len(after) + [VMEM] * len(held),
        out_specs=VMEM,
        compiler_params=params(),
        cost_estimate=cost,
        name="mark",
    )(*after, *held)


def tie(value, after, cost=LIGHT):
    def body(*refs):
        pass

    return pl.pallas_call(
        body,
        out_shape=jax.ShapeDtypeStruct(value.shape, value.dtype),
        in_specs=[ANY] * (1 + len(after)),
        out_specs=ANY,
        input_output_aliases={0: 0},
        compiler_params=params(),
        cost_estimate=cost,
        name="tie",
    )(value, *after)


def stack(pieces, after=()):
    rows, units = pieces[0].shape
    count = len(pieces)

    def body(*refs):
        for n in range(count):
            refs[-1][n * rows : (n + 1) * rows] = refs[n][...]

    return pl.pallas_call(
        body,
        out_shape=jax.ShapeDtypeStruct((count * rows, units), pieces[0].dtype),
        in_specs=[VMEM] * count + [ANY] * len(after),
        out_specs=VMEM,
        compiler_params=params(),
        cost_estimate=COST,
        name="stack",
    )(*pieces, *after)


def per_device_line(tokens, grad_out, pre_act, w_in, w_out):
    row = lax.axis_index("row")
    col = lax.axis_index("col")
    chip, core = col // 2, col % 2
    apart = [chip ^ row ^ d for d in range(4)]
    spots = [2 * (v & 1) + v // 2 for v in apart]
    place = jnp.stack(spots + [core]).astype(jnp.int32)

    units = w_out.shape[0]
    per_chunk = units // CHUNKS

    started = mark()
    for _ in range(7):
        started = mark((started,))
    w_out = pltpu.with_memory_space_constraint(w_out, pltpu.HBM)
    pre_far, pre_near = swap_chips(pre_act, 2), swap_chips(pre_act, 1)
    own0, send0, x, flipped = hidden_grad(
        [grad_out] + [swap_rows(grad_out, d) for d in (1, 2, 3)],
        w_out,
        0,
        per_chunk,
        (started,),
        place,
    )
    pre_most = stack([pre_act, pre_far, pre_near], (send0,))
    step = mark((pre_most,), COST)
    held0, out0 = add_halves(own0, swap_cores(send0), (step,))
    own1, send1 = hidden_grad([flipped], w_out, per_chunk, per_chunk, (out0,))
    mine = stack([tokens], (send1,))
    mine0, out0, held1, out1 = sum_near(
        held0, swap_chips(out0, 1), own1, swap_cores(send1), (mine,)
    )
    pre_own = stack([pre_act, pre_far, pre_near, swap_chips(pre_far, 1)], (out1,))
    pre = [pre_own, swap_cores(pre_own)]
    grad0 = far_slope(mine0, swap_chips(out0, 2), pre_act, 0, (pre_own,), COST)
    mine1, out1 = add_halves(held1, swap_chips(out1, 1), (grad0,), LIGHT)
    ends = [units * n // 12 for n in (0, 2, 7, 12)]
    parts = [b - a for a, b in zip(ends[:-1], ends[1:])]
    grad_w_out, token = weight_grad(pre, x, 0, 0, parts[0], units, None, True, (out1,), LIGHT)
    pair0 = stack([grad0, swap_chips(grad0, 2)], (token,))
    grad_w_out, token = weight_grad(
        pre, x, 0, ends[1], parts[1], units, grad_w_out, True, (pair0,)
    )
    tok = join_rows([mine] + [swap_rows(mine, d) for d in (1, 2, 3)], place, (token,))
    grad1 = far_slope(mine1, swap_chips(out1, 2), pre_act, 1, (tok,))
    near0 = tie(swap_chips(pair0, 1), (grad1,))
    whole = [pair0, near0, swap_cores(pair0), swap_cores(near0)]
    step = mark((near0,), LIGHT, (w_in,))
    grad_w_in, token = weight_grad(
        whole, tok, 0, 0, per_chunk, units, None, False, (step,), LIGHT
    )
    pair1 = stack([grad1, swap_chips(grad1, 2)], (token,))
    grad_w_out, token = weight_grad(
        pre, x, 0, ends[2], parts[2], units, grad_w_out, True, (pair1,), LIGHT
    )
    (total,) = token_grad(whole, w_in, 0, None, None, (token,))
    near1 = tie(swap_chips(pair1, 1), (total,))
    whole = [pair1, near1, swap_cores(pair1), swap_cores(near1)]
    part, *parts = token_grad(whole, w_in, per_chunk, total, place)
    grad_w_in, _ = weight_grad(
        whole, tok, per_chunk, 0, per_chunk, units, grad_w_in, False, (part,)
    )
    for d in (1, 2, 3):
        part = part + swap_rows(parts[d - 1], d).astype(jnp.float32)
    return (part.astype(jnp.bfloat16), grad_w_in, grad_w_out)


def solution(mesh):
    line = mesh.shape["row"] == 4 and mesh.shape["col"] == 8
    in_specs = (P("row", "col"), P("row", "col"), P("col", "row"), P("row", "col"), P("row", "col"))
    out_specs = (P("row", "col"), P("row", "col"), P("row", "col"))
    return jax.shard_map(
        per_device_line if line else per_device_any,
        mesh=mesh,
        in_specs=in_specs,
        out_specs=out_specs,
        check_vma=False,
    )
```
